1024 devices in a mesh: node: 64 (over y, x, core), local: 16 (over z).
Axes of the slice: x: 4, y: 8, z: 16, core: 2. Of those that a mesh axis runs over, the one named last changes fastest.
Arguments:
- tokens: bfloat16 [2048, 7168], P('node', 'local'), may hold values from -6 to 6
- cotangent: bfloat16 [2048, 7168], P('node', 'local'), may hold values from -1.5 to 1.5
- routes: int32 [2048, 8], P('node'), may hold values from 0 to 63, all different within a row; in each aligned block of 32 rows (0 to 31, 32 to 63, ...) at most 8 rows name the same one
- gate_probs: float32 [2048, 8], P('node'), may hold values from 0.1 to 1
- w_in: bfloat16 [64, 7168, 1024], P('node', 'local'), may hold values from -0.0625 to 0.0625
- w_out: bfloat16 [64, 1024, 7168], P('node', None, 'local'), may hold values from -0.1875 to 0.1875
Outputs:
- mixed: bfloat16 [2048, 7168], P('node', 'local')
- d_tokens: bfloat16 [2048, 7168], P('node', 'local')
- d_gates: float32 [2048, 8], P('node')
The draws below stay inside these ranges and needn't reach their ends.
Inputs may be any that keep to these rules, and one draw needn't show every extreme that they name: `routes`: each row names 8 different experts. In each block of 32 rows (rows 0 to 31, and so on), no expert is named by more than 8 rows, a bound that some block reaches.
All inputs are finite; a program needn't handle non-finite values.
Results may differ from the reference program's by a relative error of at most 0.03.
Values may be sent and summed in bfloat16 or wider, within the bound.
No kernel may reach another device: no remote copies, remote signals or barrier semaphores. Data moves between devices by JAX's collectives and lax.ppermute only.
A program may use at most 32 MiB of HBM per device.

```python
import math
import jax
import jax.numpy as jnp
import numpy as np
from jax import lax

D = 7168
TOP = 8
HID = 1024
TOK_NODE = 32
EXPERTS = 64
CAP = 8
TOKENS = 2048
N_NODE = 64
N_LOCAL = 16


def block_scale(key, extent, pieces, least, top_value):
    level = 1.0
    for axis_at, parts in pieces:
        draws = jax.random.uniform(jax.random.fold_in(jax.random.fold_in(key, 6), axis_at), (parts,), jnp.float32, least / len(pieces), top_value / len(pieces))
        level = level * jnp.repeat(jnp.exp(draws), extent[axis_at] // parts).reshape((-1,) + (1,) * (len(extent) - 1 - axis_at))
    return level


def deal_out(key, own, number, rows, count, top, bound, skew):
    ranking = jax.random.permutation(key, count)
    crowded, usual = load_shares(count, rows * top, bound, skew, True), load_shares(count, rows * top, bound, skew, False)
    places = jnp.arange(count)

    def named(sizes, offset_by):
        used = int((sizes > 0).sum())
        fixed = max(1, used // 4)
        shifted = fixed + (places - fixed + offset_by * (used - fixed)) % max(1, count - fixed)
        return jnp.zeros((count,), jnp.int32).at[ranking[jnp.where(places < fixed, places, shifted)]].set(jnp.asarray(sizes, jnp.int32))

    sizes = jnp.where(number % 4 == 0, named(crowded, number // 4), named(usual, number - number // 4 - 1))
    mixed = jax.random.permutation(jax.random.fold_in(own, 3), count)
    source_of, sink = mixed[0:count // 2 * 2:2], mixed[1:count // 2 * 2:2]
    room = jnp.minimum(sizes[source_of] - 1, bound - sizes[sink]) // 2
    room = jnp.where((source_of == ranking[0]) | (sink == ranking[0]) | (sizes[sink] == 0), 0, jnp.maximum(room, 0))
    shifted = jax.random.randint(jax.random.fold_in(own, 4), (count // 2,), 0, 1 << 20) % (room + 1)
    sizes = sizes.at[source_of].add(-shifted).at[sink].add(shifted)
    labels = jnp.searchsorted(jnp.cumsum(sizes), jnp.arange(rows * top), side="right").astype(jnp.int32)
    grid = labels.reshape(top, rows).T
    grid = grid[jax.random.permutation(jax.random.fold_in(own, 1), rows)]
    offset_by = jax.random.randint(jax.random.fold_in(own, 2), (rows, 1), 0, top)
    return jnp.take_along_axis(grid, (jnp.arange(top)[None, :] + offset_by) % top, axis=1)


def load_shares(number_of, total, limit, slope, full):
    portions = [(1 << 20) // math.isqrt(rank ** slope) + 1 for rank in range(1, number_of + 1)]
    largest = limit if full else min(limit, max(-(-total // number_of), total * portions[0] // sum(portions)))
    least = 1 if total - largest >= number_of - 1 else 0
    given, spare = [largest] + [least] * (number_of - 1), total - largest - least * (number_of - 1)
    while spare > 0:
        candidates = [i for i in range(1, number_of) if given[i] < largest] or [i for i in range(1, number_of) if given[i] < limit]
        whole, remaining = sum([portions[i] for i in candidates]), spare
        for i in candidates:
            extra = min(limit - given[i], max(1, remaining * portions[i] // whole), spare)
            given[i] = given[i] + extra
            spare = spare - extra
    return np.array(given)


def gaussian(rng, shape, width, bound, split=(), kind=jnp.bfloat16):
    loudness = block_scale(rng, shape, split, -0.22, 0.18) if split else 1.0
    entries = jax.random.normal(rng, shape, jnp.float32) * width * loudness
    return jnp.minimum(jnp.maximum(entries, -bound), bound).astype(kind)


def setup_inputs(seed: int = 0) -> dict:
    streams_of = jax.random.split(jax.random.key(seed), 7)
    tokens = gaussian(streams_of[0], (TOKENS, D), 1.0, 6.0, ((0, 64), (1, 16)))
    cotangent = gaussian(streams_of[1], (TOKENS, D), 0.25, 1.5, ((0, 64), (1, 16)))
    routes_keys = jax.random.split(jax.random.fold_in(streams_of[2], 1), TOKENS // TOK_NODE)
    routes_turns = jax.random.permutation(jax.random.fold_in(streams_of[2], 3), TOKENS // TOK_NODE)
    routes = jax.vmap(lambda own, number: deal_out(jax.random.fold_in(streams_of[2], 2), own, number, TOK_NODE, EXPERTS, TOP, CAP, 2))(routes_keys, routes_turns).reshape((TOKENS, TOP))
    gate_probs = jnp.clip(0.1 + 0.9 * jax.random.uniform(streams_of[3], (TOKENS, TOP), jnp.float32) ** block_scale(streams_of[3], (TOKENS, TOP), ((0, 64),), -0.2, 0.2), 0.1, 1.0)
    w_in = gaussian(streams_of[4], (EXPERTS, D, HID), D ** -0.5, 0.0625, ((0, 64), (1, 16)))
    w_out = gaussian(streams_of[5], (EXPERTS, HID, D), HID ** -0.5, 0.1875, ((0, 64), (2, 16)))
    return {"tokens": tokens, "cotangent": cotangent, "routes": routes, "gate_probs": gate_probs, "w_in": w_in, "w_out": w_out}


def grouped_sum(rows_data, matrix_groups, form):
    partial_value = jnp.einsum(form, rows_data, matrix_groups)
    rounded = lax.optimization_barrier(partial_value.astype(jnp.bfloat16))
    return jnp.sum(rounded.astype(jnp.float32), axis=0)


def reference(tokens, cotangent, routes, gate_probs, w_in, w_out):
    row_total = N_NODE * CAP
    feature_part = D // N_LOCAL
    expert_ids = jnp.arange(EXPERTS, dtype=jnp.int32)
    matches = (routes[:, :, None] == expert_ids[None, None, :]).astype(jnp.int32)
    hits = jnp.sum(matches, axis=1).reshape(N_NODE, TOK_NODE, EXPERTS)
    before = (jnp.cumsum(hits, axis=1) - hits).reshape(TOKENS, EXPERTS)
    slot_index = jnp.sum(matches * before[:, None, :], axis=2).astype(jnp.int32)
    token_ids = jnp.arange(TOKENS, dtype=jnp.int32)
    row_of = ((token_ids // TOK_NODE)[:, None] * CAP + slot_index).astype(jnp.int32)
    where_to = (routes * row_total + row_of).reshape(-1).astype(jnp.int32)
    table = jnp.full((EXPERTS * row_total,), TOKENS, jnp.int32)
    table = table.at[where_to].set(jnp.repeat(token_ids, TOP)).reshape(EXPERTS, row_total)
    blank = jnp.zeros((1, D), jnp.bfloat16)
    token_pad = jnp.concatenate([tokens, blank], axis=0)
    cot_pad = jnp.concatenate([cotangent, blank], axis=0)
    cot_float = cotangent.astype(jnp.float32)

    def expert_pass(carry, inputs):
        mixed_acc, dtok_acc, gates_acc = carry
        index, w_up, w_down, ident = inputs
        x_rows = token_pad[index].astype(jnp.float32).reshape(row_total, N_LOCAL, feature_part)
        dy_rows = cot_pad[index].astype(jnp.float32).reshape(row_total, N_LOCAL, feature_part)
        up_groups = w_up.astype(jnp.float32).reshape(N_LOCAL, feature_part, HID)
        down_groups = w_down.astype(jnp.float32).reshape(HID, N_LOCAL, feature_part)
        pre = grouped_sum(x_rows, up_groups, "rjd,jdh->jrh")
        act = jax.nn.silu(pre).astype(jnp.bfloat16)
        out = jnp.dot(act, w_down, preferred_element_type=jnp.float32).astype(jnp.bfloat16)
        dact = grouped_sum(dy_rows, down_groups, "rjd,hjd->jrh")
        sig = jax.nn.sigmoid(pre)
        dpre = (dact * sig * (1.0 + pre * (1.0 - sig))).astype(jnp.bfloat16)
        dout = jnp.dot(dpre, w_up.T, preferred_element_type=jnp.float32).astype(jnp.bfloat16)
        picks = routes == ident
        weight = jnp.sum(jnp.where(picks, gate_probs, jnp.float32(0.0)), axis=1)
        named = jnp.any(picks, axis=1)
        row_pick = jnp.where(named, jnp.sum(jnp.where(picks, row_of, 0), axis=1), row_total).astype(jnp.int32)
        blank_row = jnp.zeros((1, D), jnp.bfloat16)
        y_tok = jnp.concatenate([out, blank_row], axis=0)[row_pick].astype(jnp.float32)
        g_tok = jnp.concatenate([dout, blank_row], axis=0)[row_pick].astype(jnp.float32)
        mixed_acc = mixed_acc + weight[:, None] * y_tok
        dtok_acc = dtok_acc + weight[:, None] * g_tok
        inner = jnp.sum(cot_float * y_tok, axis=1)
        gates_acc = gates_acc + jnp.where(picks, inner[:, None], jnp.float32(0.0))
        return (mixed_acc, dtok_acc, gates_acc), None

    start = (jnp.zeros((TOKENS, D), jnp.float32), jnp.zeros((TOKENS, D), jnp.float32), jnp.zeros((TOKENS, TOP), jnp.float32))
    (mixed, d_tokens, d_gates), unused = lax.scan(expert_pass, start, (table, w_in, w_out, expert_ids))
    return mixed.astype(jnp.bfloat16), d_tokens.astype(jnp.bfloat16), d_gates
```

```python
import functools

import jax
import jax.numpy as jnp
from jax import lax
from jax.experimental import pallas as pl
from jax.experimental.pallas import tpu as pltpu
from jax.sharding import PartitionSpec as P

BF16 = jnp.bfloat16
F32 = jnp.float32
VMEM = pl.BlockSpec(memory_space=pltpu.VMEM)
LIMIT = 48 * 1024 * 1024


def pieces(rows, cols):
    half = cols // 2
    out = []
    for r in range(0, rows, 32):
        out.append((r, 32, 0, half))
        out.append((r, 32, half, half))
    r, nr, c, nc = out.pop()
    out.append((r, nr, c, nc // 2))
    out.append((r, nr, c + nc // 2, nc // 2))
    return out


def slot_columns(routes, node_count, capacity):
    tok, top = routes.shape
    rows = node_count * capacity
    expert = lax.broadcasted_iota(jnp.int32, (tok, node_count), 1)
    hits = jnp.zeros((tok, node_count), F32)
    for k in range(top):
        hits += jnp.where(routes[:, k : k + 1] == expert, 1.0, 0.0)
    earlier = lax.broadcasted_iota(jnp.int32, (tok, tok), 1) < lax.broadcasted_iota(jnp.int32, (tok, tok), 0)
    before = jnp.dot(jnp.where(earlier, 1.0, 0.0).astype(BF16), hits.astype(BF16), preferred_element_type=F32)
    col = lax.broadcasted_iota(jnp.int32, (tok, rows), 1)
    spread = jnp.where(
        lax.broadcasted_iota(jnp.int32, (node_count, rows), 1) // capacity
        == lax.broadcasted_iota(jnp.int32, (node_count, rows), 0),
        1.0,
        0.0,
    ).astype(BF16)
    before_cols = jnp.dot(before.astype(BF16), spread, preferred_element_type=F32)
    in_slot = before_cols == (col % capacity).astype(F32)
    return col // capacity, in_slot


def pack_kernel(node_count, capacity, routes_ref, tokens_ref, cot_ref, sent_ref):
    routes = routes_ref[...]
    expert, in_slot = slot_columns(routes, node_count, capacity)
    chosen = jnp.zeros(expert.shape, F32)
    for k in range(routes.shape[1]):
        chosen += jnp.where((routes[:, k : k + 1] == expert) & in_slot, 1.0, 0.0)
    chosen = chosen.T.astype(BF16)
    both = jnp.concatenate([tokens_ref[...].astype(F32), cot_ref[...].astype(F32)], axis=1).astype(BF16)
    sent_ref[...] = jnp.dot(chosen, both, preferred_element_type=F32).astype(BF16)


def terms_kernel(parts, x_ref, w_in_ref, w_out_ref, *outs):
    feat, hidden = w_in_ref.shape
    rows = x_ref.shape[0]
    step = min(128, rows)
    pre_outs, dact_outs = outs[: len(parts)], outs[len(parts) :]
    for r0 in range(0, rows, step):
        pre = jnp.dot(x_ref[r0 : r0 + step, :feat], w_in_ref[...], preferred_element_type=F32).astype(BF16)
        dact = jnp.dot(x_ref[r0 : r0 + step, feat:], w_out_ref[...], preferred_element_type=F32).astype(BF16)
        for value, refs in ((pre, pre_outs), (dact, dact_outs)):
            for (r, nr, c, nc), ref in zip(parts, refs):
                if r0 <= r < r0 + step:
                    ref[...] = value[r - r0 : r - r0 + nr, c : c + nc]


def outputs_kernel(parts, *refs):
    count = len(parts)
    pre_refs, dact_refs = refs[:count], refs[count : 2 * count]
    w_in_ref, w_out_ref, back_ref = refs[2 * count :]
    feat = w_in_ref.shape[0]
    rows, width = back_ref.shape
    half = width // 2
    step = min(128, rows)

    def rows_of(some, r0):
        bands = []
        for r in range(r0, r0 + step, 32):
            band = [ref[...] for (pr, _, _, _), ref in zip(parts, some) if pr == r]
            bands.append(jnp.concatenate(band, axis=1))
        return jnp.concatenate(bands, axis=0).astype(F32)

    for r0 in range(0, rows, step):
        pre = rows_of(pre_refs, r0)
        dact = rows_of(dact_refs, r0)
        sig = 1.0 / (1.0 + jnp.exp(-pre))
        act = (pre * sig).astype(BF16)
        dpre = (dact * sig * (1.0 + pre * (1.0 - sig))).astype(BF16)
        inner = jnp.sum(act.astype(F32) * dact, axis=1, keepdims=True)
        hi = inner.astype(BF16).astype(F32)
        mid = (inner - hi).astype(BF16).astype(F32)
        lo = inner - hi - mid
        y = lax.dot_general(act, w_out_ref[...], (((1,), (1,)), ((), ())), preferred_element_type=F32)
        dout = lax.dot_general(dpre, w_in_ref[...], (((1,), (1,)), ((), ())), preferred_element_type=F32)
        lane = lax.broadcasted_iota(jnp.int32, (step, half - feat), 1)
        extra = jnp.where(lane == 0, hi, jnp.where(lane == 1, mid, jnp.where(lane == 2, lo, 0.0)))
        back_ref[r0 : r0 + step, :feat] = y.astype(BF16)
        back_ref[r0 : r0 + step, feat:half] = extra.astype(BF16)
        back_ref[r0 : r0 + step, half : half + feat] = dout.astype(BF16)
        back_ref[r0 : r0 + step, half + feat :] = jnp.zeros((step, half - feat), BF16)


def unpack_kernel(node_count, capacity, routes_ref, gates_ref, back_ref, mixed_ref, d_tokens_ref, d_gates_ref):
    routes = routes_ref[...]
    gates = gates_ref[...]
    tok, top = routes.shape
    feat = mixed_ref.shape[1]
    half = back_ref.shape[1] // 2
    expert, in_slot = slot_columns(routes, node_count, capacity)
    weight = jnp.zeros(expert.shape, F32)
    picks = []
    for k in range(top):
        mine = (routes[:, k : k + 1] == expert) & in_slot
        weight += jnp.where(mine, gates[:, k : k + 1], 0.0)
        picks.append(jnp.where(mine, 1.0, 0.0).astype(BF16))
    hi = weight.astype(BF16)
    rest = weight - hi.astype(F32)
    mid = rest.astype(BF16)
    lo = (rest - mid.astype(F32)).astype(BF16)
    stack = jnp.concatenate([hi, mid, lo], axis=0)
    out = jnp.dot(stack, back_ref[...], preferred_element_type=F32)
    out = out[:tok] + (out[tok : 2 * tok] + out[2 * tok :])
    mixed_ref[...] = out[:, :feat].astype(BF16)
    d_tokens_ref[...] = out[:, half : half + feat].astype(BF16)
    tail = half - 128
    lane = lax.broadcasted_iota(jnp.int32, (1, 128), 1)
    column = lax.broadcasted_iota(jnp.int32, (tok, top), 1)
    d_gates = jnp.zeros((tok, top), F32)
    for k in range(top):
        got = jnp.dot(picks[k], back_ref[:, tail:half], preferred_element_type=F32)
        value = jnp.sum(jnp.where(lane >= feat - tail, got, 0.0), axis=1, keepdims=True)
        d_gates = jnp.where(column == k, value, d_gates)
    d_gates_ref[...] = d_gates


def call(kernel, count, out_shape, *args):
    return pl.pallas_call(
        kernel,
        out_shape=out_shape,
        in_specs=[VMEM] * count,
        out_specs=jax.tree.map(lambda _: VMEM, out_shape),
        compiler_params=pltpu.CompilerParams(vmem_limit_bytes=LIMIT),
    )(*args)


def body(tokens, cotangent, routes, gate_probs, w_in, w_out):
    tok, feat = tokens.shape
    top = routes.shape[1]
    nodes = lax.axis_size("node")
    hidden = w_in.shape[2]
    capacity = min(tok, 2 * tok * top // nodes)
    rows = nodes * capacity
    width = 2 * (-(-(feat + 3) // 128) * 128)
    parts = pieces(rows, hidden)
    up, down = w_in[0], w_out[0].T

    def exchange(values):
        return lax.all_to_all(
            values.reshape(nodes, capacity, values.shape[1]), "node", split_axis=0, concat_axis=0, tiled=True
        ).reshape(rows, values.shape[1])

    sent = call(
        functools.partial(pack_kernel, nodes, capacity),
        3,
        jax.ShapeDtypeStruct((rows, 2 * feat), BF16),
        routes,
        tokens,
        cotangent,
    )
    x_dy = exchange(sent)
    terms = call(
        functools.partial(terms_kernel, parts),
        3,
        tuple(jax.ShapeDtypeStruct((nr, nc), BF16) for _, nr, _, nc in parts) * 2,
        x_dy,
        up,
        down,
    )
    sums = lax.psum(tuple(terms), "local")
    back = call(
        functools.partial(outputs_kernel, parts),
        len(sums) + 2,
        jax.ShapeDtypeStruct((rows, width), BF16),
        *sums,
        up,
        down,
    )
    returned = exchange(back)
    return call(
        functools.partial(unpack_kernel, nodes, capacity),
        3,
        (
            jax.ShapeDtypeStruct((tok, feat), BF16),
            jax.ShapeDtypeStruct((tok, feat), BF16),
            jax.ShapeDtypeStruct((tok, top), F32),
        ),
        routes,
        gate_probs,
        returned,
    )


def solution(mesh):
    in_specs = (
        P("node", "local"),
        P("node", "local"),
        P("node", None),
        P("node", None),
        P("node", "local", None),
        P("node", None, "local"),
    )
    out_specs = (P("node", "local"), P("node", "local"), P("node", None))
    return jax.shard_map(body, mesh=mesh, in_specs=in_specs, out_specs=out_specs, check_vma=False)
```

```python
import functools

import jax
import jax.numpy as jnp
from jax import lax
from jax.experimental import pallas as pl
from jax.experimental.pallas import tpu as pltpu
from jax.sharding import PartitionSpec as P

BF16 = jnp.bfloat16
F32 = jnp.float32
VMEM = pl.BlockSpec(memory_space=pltpu.VMEM)
HBM = pl.BlockSpec(memory_space=pltpu.HBM)
LARGE = 60 * 1024 * 1024
SMALL = 16 * 1024 * 1024


def pieces(rows, cols):
    half = cols // 2
    out = []
    for r in range(0, rows, 32):
        out.append((r, 32, 0, half))
        out.append((r, 32, half, half))
    r, nr, c, nc = out.pop()
    out.append((r, nr, c, nc // 2))
    out.append((r, nr, c + nc // 2, nc // 2))
    return out


def slot_columns(routes, node_count, capacity):
    tok, top = routes.shape
    rows = node_count * capacity
    expert = lax.broadcasted_iota(jnp.int32, (tok, node_count), 1)
    hits = jnp.zeros((tok, node_count), F32)
    for k in range(top):
        hits += jnp.where(routes[:, k : k + 1] == expert, 1.0, 0.0)
    earlier = lax.broadcasted_iota(jnp.int32, (tok, tok), 1) < lax.broadcasted_iota(jnp.int32, (tok, tok), 0)
    before = jnp.dot(jnp.where(earlier, 1.0, 0.0).astype(BF16), hits.astype(BF16), preferred_element_type=F32)
    col = lax.broadcasted_iota(jnp.int32, (tok, rows), 1)
    spread = jnp.where(
        lax.broadcasted_iota(jnp.int32, (node_count, rows), 1) // capacity
        == lax.broadcasted_iota(jnp.int32, (node_count, rows), 0),
        1.0,
        0.0,
    ).astype(BF16)
    before_cols = jnp.dot(before.astype(BF16), spread, preferred_element_type=F32)
    in_slot = before_cols == (col % capacity).astype(F32)
    return col // capacity, in_slot


def pack_kernel(node_count, capacity, routes_ref, tokens_ref, cot_ref, sent_ref):
    routes = routes_ref[...]
    expert, in_slot = slot_columns(routes, node_count, capacity)
    chosen = jnp.zeros(expert.shape, F32)
    for k in range(routes.shape[1]):
        chosen += jnp.where((routes[:, k : k + 1] == expert) & in_slot, 1.0, 0.0)
    chosen = chosen.T.astype(BF16)
    both = jnp.concatenate([tokens_ref[...].astype(F32), cot_ref[...].astype(F32)], axis=1).astype(BF16)
    sent_ref[...] = jnp.dot(chosen, both, preferred_element_type=F32).astype(BF16)


def terms_kernel(parts, x_ref, w_in_ref, w_out_ref, *refs):
    count = len(parts)
    outs, (pre_ref, dact_ref, sems) = refs[: 2 * count], refs[2 * count :]
    feat = w_in_ref.shape[0]
    rows = x_ref.shape[0]
    step = min(128, rows)
    copies = []
    for r0 in range(0, rows, step):
        band = slice(r0, r0 + step)
        pre_ref[band] = jnp.dot(x_ref[band, :feat], w_in_ref[...], preferred_element_type=F32).astype(BF16)
        dact_ref[band] = jnp.dot(x_ref[band, feat:], w_out_ref[...], preferred_element_type=F32).astype(BF16)
        for first, source in ((0, pre_ref), (count, dact_ref)):
            for i, (r, nr, c, nc) in enumerate(parts):
                if r0 <= r < r0 + step:
                    copy = pltpu.make_async_copy(
                        source.at[pl.ds(r, nr), pl.ds(c, nc)], outs[first + i], sems.at[first + i]
                    )
                    copy.start()
                    copies.append(copy)
    for copy in copies:
        copy.wait()


def outputs_kernel(parts, *refs):
    count = len(parts)
    sums = refs[: 2 * count]
    w_in_ref, w_out_ref, back_ref, pre_ref, dact_ref, sems = refs[2 * count :]
    feat = w_in_ref.shape[0]
    rows, width = back_ref.shape
    half = width // 2
    step = min(128, rows)
    copies = []
    for i, (r, nr, c, nc) in enumerate(parts):
        for first, target in ((0, pre_ref), (count, dact_ref)):
            copy = pltpu.make_async_copy(sums[first + i], target.at[pl.ds(r, nr), pl.ds(c, nc)], sems.at[first + i])
            copy.start()
            copies.append((r, copy))

    for r0 in range(0, rows, step):
        for r, copy in copies:
            if r0 <= r < r0 + step:
                copy.wait()
        band = slice(r0, r0 + step)
        pre = pre_ref[band].astype(F32)
        dact = dact_ref[band].astype(F32)
        sig = 1.0 / (1.0 + jnp.exp(-pre))
        act = (pre * sig).astype(BF16)
        dpre = (dact * sig * (1.0 + pre * (1.0 - sig))).astype(BF16)
        inner = jnp.sum(act.astype(F32) * dact, axis=1, keepdims=True)
        hi = inner.astype(BF16).astype(F32)
        mid = (inner - hi).astype(BF16).astype(F32)
        lo = inner - hi - mid
        y = lax.dot_general(act, w_out_ref[...], (((1,), (1,)), ((), ())), preferred_element_type=F32)
        dout = lax.dot_general(dpre, w_in_ref[...], (((1,), (1,)), ((), ())), preferred_element_type=F32)
        lane = lax.broadcasted_iota(jnp.int32, (step, half - feat), 1)
        extra = jnp.where(lane == 0, hi, jnp.where(lane == 1, mid, jnp.where(lane == 2, lo, 0.0)))
        back_ref[band, :feat] = y.astype(BF16)
        back_ref[band, feat:half] = extra.astype(BF16)
        back_ref[band, half : half + feat] = dout.astype(BF16)
        back_ref[band, half + feat :] = jnp.zeros((step, half - feat), BF16)


def unpack_kernel(node_count, capacity, routes_ref, gates_ref, back_ref, mixed_ref, d_tokens_ref, d_gates_ref):
    routes = routes_ref[...]
    gates = gates_ref[...]
    tok, top = routes.shape
    feat = mixed_ref.shape[1]
    half = back_ref.shape[1] // 2
    expert, in_slot = slot_columns(routes, node_count, capacity)
    weight = jnp.zeros(expert.shape, F32)
    picks = []
    for k in range(top):
        mine = (routes[:, k : k + 1] == expert) & in_slot
        weight += jnp.where(mine, gates[:, k : k + 1], 0.0)
        picks.append(jnp.where(mine, 1.0, 0.0).astype(BF16))
    hi = weight.astype(BF16)
    rest = weight - hi.astype(F32)
    mid = rest.astype(BF16)
    lo = (rest - mid.astype(F32)).astype(BF16)
    stack = jnp.concatenate([hi, mid, lo], axis=0)
    out = jnp.dot(stack, back_ref[...], preferred_element_type=F32)
    out = out[:tok] + (out[tok : 2 * tok] + out[2 * tok :])
    mixed_ref[...] = out[:, :feat].astype(BF16)
    d_tokens_ref[...] = out[:, half : half + feat].astype(BF16)
    tail = half - 128
    lane = lax.broadcasted_iota(jnp.int32, (1, 128), 1)
    column = lax.broadcasted_iota(jnp.int32, (tok, top), 1)
    d_gates = jnp.zeros((tok, top), F32)
    for k in range(top):
        got = jnp.dot(picks[k], back_ref[:, tail:half], preferred_element_type=F32)
        value = jnp.sum(jnp.where(lane >= feat - tail, got, 0.0), axis=1, keepdims=True)
        d_gates = jnp.where(column == k, value, d_gates)
    d_gates_ref[...] = d_gates


def call(kernel, in_specs, out_shape, out_space, *args, scratch=(), limit=SMALL):
    return pl.pallas_call(
        kernel,
        out_shape=out_shape,
        in_specs=in_specs,
        out_specs=jax.tree.map(lambda _: out_space, out_shape),
        scratch_shapes=scratch,
        compiler_params=pltpu.CompilerParams(vmem_limit_bytes=limit),
    )(*args)


def body(tokens, cotangent, routes, gate_probs, w_in, w_out):
    tok, feat = tokens.shape
    top = routes.shape[1]
    nodes = lax.axis_size("node")
    hidden = w_in.shape[2]
    capacity = min(tok, 2 * tok * top // nodes)
    rows = nodes * capacity
    width = 2 * (-(-(feat + 3) // 128) * 128)
    parts = pieces(rows, hidden)
    up, down = w_in[0], w_out[0].T
    scratch = [pltpu.VMEM((rows, hidden), BF16)] * 2 + [pltpu.SemaphoreType.DMA((2 * len(parts),))]

    def exchange(values):
        return lax.all_to_all(
            values.reshape(nodes, capacity, values.shape[1]), "node", split_axis=0, concat_axis=0, tiled=True
        ).reshape(rows, values.shape[1])

    sent = call(
        functools.partial(pack_kernel, nodes, capacity),
        [VMEM] * 3,
        jax.ShapeDtypeStruct((rows, 2 * feat), BF16),
        VMEM,
        routes,
        tokens,
        cotangent,
    )
    x_dy = exchange(sent)
    terms = call(
        functools.partial(terms_kernel, parts),
        [VMEM] * 3,
        tuple(jax.ShapeDtypeStruct((nr, nc), BF16) for _, nr, _, nc in parts) * 2,
        HBM,
        x_dy,
        up,
        down,
        scratch=scratch,
        limit=LARGE,
    )
    sums = lax.psum(tuple(terms), "local")
    back = call(
        functools.partial(outputs_kernel, parts),
        [HBM] * len(sums) + [VMEM] * 2,
        jax.ShapeDtypeStruct((rows, width), BF16),
        VMEM,
        *sums,
        up,
        down,
        scratch=scratch,
        limit=LARGE,
    )
    returned = exchange(back)
    return call(
        functools.partial(unpack_kernel, nodes, capacity),
        [VMEM] * 3,
        (
            jax.ShapeDtypeStruct((tok, feat), BF16),
            jax.ShapeDtypeStruct((tok, feat), BF16),
            jax.ShapeDtypeStruct((tok, top), F32),
        ),
        VMEM,
        routes,
        gate_probs,
        returned,
    )


def solution(mesh):
    in_specs = (
        P("node", "local"),
        P("node", "local"),
        P("node", None),
        P("node", None),
        P("node", "local", None),
        P("node", None, "local"),
    )
    out_specs = (P("node", "local"), P("node", "local"), P("node", None))
    return jax.shard_map(body, mesh=mesh, in_specs=in_specs, out_specs=out_specs, check_vma=False)
```

```python
import functools

import jax
import jax.numpy as jnp
from jax import lax
from jax.experimental import pallas as pl
from jax.experimental.pallas import tpu as pltpu
from jax.sharding import PartitionSpec as P

BF16 = jnp.bfloat16
F32 = jnp.float32
VMEM = pl.BlockSpec(memory_space=pltpu.VMEM)
HBM = pl.BlockSpec(memory_space=pltpu.HBM)


def pieces(rows, cols):
    half = cols // 2
    out = []
    for r in range(0, rows, 32):
        out.append((r, 32, 0, half))
        out.append((r, 32, half, half))
    r, nr, c, nc = out.pop()
    out.append((r, nr, c, nc // 2))
    out.append((r, nr, c + nc // 2, nc // 2))
    return out


def slot_columns(routes, node_count, capacity):
    tok, top = routes.shape
    rows = node_count * capacity
    expert = lax.broadcasted_iota(jnp.int32, (tok, node_count), 1)
    hits = jnp.zeros((tok, node_count), F32)
    for k in range(top):
        hits += jnp.where(routes[:, k : k + 1] == expert, 1.0, 0.0)
    earlier = lax.broadcasted_iota(jnp.int32, (tok, tok), 1) < lax.broadcasted_iota(jnp.int32, (tok, tok), 0)
    before = jnp.dot(jnp.where(earlier, 1.0, 0.0).astype(BF16), hits.astype(BF16), preferred_element_type=F32)
    col = lax.broadcasted_iota(jnp.int32, (tok, rows), 1)
    spread = jnp.where(
        lax.broadcasted_iota(jnp.int32, (node_count, rows), 1) // capacity
        == lax.broadcasted_iota(jnp.int32, (node_count, rows), 0),
        1.0,
        0.0,
    ).astype(BF16)
    before_cols = jnp.dot(before.astype(BF16), spread, preferred_element_type=F32)
    in_slot = before_cols == (col % capacity).astype(F32)
    return col // capacity, in_slot


def pack_kernel(node_count, capacity, routes_ref, tokens_ref, cot_ref, sent_ref, tokens_buf, cot_buf, sems):
    copies = [
        pltpu.make_async_copy(tokens_ref, tokens_buf, sems.at[0]),
        pltpu.make_async_copy(cot_ref, cot_buf, sems.at[1]),
    ]
    for copy in copies:
        copy.start()
    routes = routes_ref[...].T
    expert, in_slot = slot_columns(routes, node_count, capacity)
    chosen = jnp.zeros(expert.shape, F32)
    for k in range(routes.shape[1]):
        chosen += jnp.where((routes[:, k : k + 1] == expert) & in_slot, 1.0, 0.0)
    chosen = chosen.T.astype(BF16)
    for copy in copies:
        copy.wait()
    both = jnp.concatenate([tokens_buf[...].astype(F32), cot_buf[...].astype(F32)], axis=1).astype(BF16)
    sent_ref[...] = jnp.dot(chosen, both, preferred_element_type=F32).astype(BF16)


def terms_kernel(parts, x_ref, w_in_hbm, w_out_hbm, *refs):
    outs, (w_in_ref, w_out_ref, sems) = refs[: 2 * len(parts)], refs[2 * len(parts) :]
    weights = [
        pltpu.make_async_copy(w_in_hbm, w_in_ref, sems.at[0]),
        pltpu.make_async_copy(w_out_hbm, w_out_ref, sems.at[1]),
    ]
    for copy in weights:
        copy.start()
    feat = w_in_ref.shape[0]
    rows = x_ref.shape[0]
    step = min(128, rows)
    for r0 in range(0, rows, step):
        band = slice(r0, r0 + step)
        if r0 == 0:
            weights[0].wait()
        pre = jnp.dot(x_ref[band, :feat], w_in_ref[...], preferred_element_type=F32).astype(BF16)
        if r0 == 0:
            weights[1].wait()
        dact = jnp.dot(x_ref[band, feat:], w_out_ref[...], preferred_element_type=F32).astype(BF16)
        for value, refs in ((pre, outs[: len(parts)]), (dact, outs[len(parts) :])):
            for (r, nr, c, nc), ref in zip(parts, refs):
                if r0 <= r < r0 + step:
                    ref[...] = value[r - r0 : r - r0 + nr, c : c + nc]


def outputs_kernel(parts, *refs):
    count = len(parts)
    sums = refs[: 2 * count]
    w_in_hbm, w_out_hbm, back_ref, pre_ref, dact_ref, w_in_ref, w_out_ref, sems = refs[2 * count :]
    feat = w_in_ref.shape[0]
    rows, width = back_ref.shape
    half = width // 2
    step = min(128, rows)
    copies = []
    for i, (r, nr, c, nc) in enumerate(parts):
        for first, target in ((0, pre_ref), (count, dact_ref)):
            copy = pltpu.make_async_copy(sums[first + i], target.at[pl.ds(r, nr), pl.ds(c, nc)], sems.at[first + i])
            copy.start()
            copies.append((r, copy))
    weights = [
        pltpu.make_async_copy(w_in_hbm, w_in_ref, sems.at[2 * count]),
        pltpu.make_async_copy(w_out_hbm, w_out_ref, sems.at[2 * count + 1]),
    ]
    for copy in weights:
        copy.start()

    for r0 in range(0, rows, step):
        for r, copy in copies:
            if r0 <= r < r0 + step:
                copy.wait()
        band = slice(r0, r0 + step)
        pre = pre_ref[band].astype(F32)
        dact = dact_ref[band].astype(F32)
        sig = 1.0 / (1.0 + jnp.exp(-pre))
        act = (pre * sig).astype(BF16)
        dpre = (dact * sig * (1.0 + pre * (1.0 - sig))).astype(BF16)
        inner = jnp.sum(act.astype(F32) * dact, axis=1, keepdims=True)
        hi = inner.astype(BF16).astype(F32)
        mid = (inner - hi).astype(BF16).astype(F32)
        lo = inner - hi - mid
        if r0 == 0:
            for copy in weights:
                copy.wait()
        y = lax.dot_general(act, w_out_ref[...], (((1,), (1,)), ((), ())), preferred_element_type=F32)
        dout = lax.dot_general(dpre, w_in_ref[...], (((1,), (1,)), ((), ())), preferred_element_type=F32)
        lane = lax.broadcasted_iota(jnp.int32, (step, half - feat), 1)
        extra = jnp.where(lane == 0, hi, jnp.where(lane == 1, mid, jnp.where(lane == 2, lo, 0.0)))
        back_ref[band, :feat] = y.astype(BF16)
        back_ref[band, feat:half] = extra.astype(BF16)
        back_ref[band, half : half + feat] = dout.astype(BF16)
        back_ref[band, half + feat :] = jnp.zeros((step, half - feat), BF16)


def unpack_kernel(node_count, capacity, routes_ref, gates_ref, back_ref, mixed_ref, d_tokens_ref, d_gates_ref):
    routes = routes_ref[...].T
    gates = gates_ref[...].T
    tok, top = routes.shape
    feat = mixed_ref.shape[1]
    half = back_ref.shape[1] // 2
    expert, in_slot = slot_columns(routes, node_count, capacity)
    weight = jnp.zeros(expert.shape, F32)
    picks = []
    for k in range(top):
        mine = (routes[:, k : k + 1] == expert) & in_slot
        weight += jnp.where(mine, gates[:, k : k + 1], 0.0)
        picks.append(jnp.where(mine, 1.0, 0.0).astype(BF16))
    hi = weight.astype(BF16)
    rest = weight - hi.astype(F32)
    mid = rest.astype(BF16)
    lo = (rest - mid.astype(F32)).astype(BF16)
    stack = jnp.concatenate([hi, mid, lo], axis=0)
    out = jnp.dot(stack, back_ref[...], preferred_element_type=F32)
    out = out[:tok] + (out[tok : 2 * tok] + out[2 * tok :])
    mixed_ref[...] = out[:, :feat].astype(BF16)
    d_tokens_ref[...] = out[:, half : half + feat].astype(BF16)
    tail = half - 128
    lane = lax.broadcasted_iota(jnp.int32, (1, 128), 1)
    column = lax.broadcasted_iota(jnp.int32, (tok, top), 1)
    d_gates = jnp.zeros((tok, top), F32)
    for k in range(top):
        got = jnp.dot(picks[k], back_ref[:, tail:half], preferred_element_type=F32)
        value = jnp.sum(jnp.where(lane >= feat - tail, got, 0.0), axis=1, keepdims=True)
        d_gates = jnp.where(column == k, value, d_gates)
    d_gates_ref[...] = d_gates.T


def call(kernel, in_specs, out_shape, *args, scratch=(), limit=16):
    return pl.pallas_call(
        kernel,
        out_shape=out_shape,
        in_specs=in_specs,
        out_specs=jax.tree.map(lambda _: VMEM, out_shape),
        scratch_shapes=scratch,
        compiler_params=pltpu.CompilerParams(vmem_limit_bytes=limit * 1024 * 1024),
    )(*args)


def in_hbm(*arrays):
    return [pltpu.with_memory_space_constraint(array, pltpu.HBM) for array in arrays]


def body(tokens, cotangent, routes, gate_probs, w_in, w_out):
    tok, feat = tokens.shape
    top = routes.shape[1]
    nodes = lax.axis_size("node")
    hidden = w_in.shape[2]
    capacity = min(tok, 2 * tok * top // nodes)
    rows = nodes * capacity
    width = 2 * (-(-(feat + 3) // 128) * 128)
    parts = pieces(rows, hidden)
    up, down = w_in[0], w_out[0].T
    routes_t = routes.T

    def exchange(values):
        return lax.all_to_all(
            values.reshape(nodes, capacity, values.shape[1]), "node", split_axis=0, concat_axis=0, tiled=True
        ).reshape(rows, values.shape[1])

    sent = call(
        functools.partial(pack_kernel, nodes, capacity),
        [VMEM, HBM, HBM],
        jax.ShapeDtypeStruct((rows, 2 * feat), BF16),
        routes_t,
        *in_hbm(tokens, cotangent),
        scratch=[pltpu.VMEM((tok, feat), BF16)] * 2 + [pltpu.SemaphoreType.DMA((2,))],
    )
    x_dy = exchange(sent)
    terms = call(
        functools.partial(terms_kernel, parts),
        [VMEM, HBM, HBM],
        tuple(pltpu.VMEM((nr, nc), BF16) for _, nr, _, nc in parts) * 2,
        x_dy,
        *in_hbm(up, down),
        scratch=[pltpu.VMEM((feat, hidden), BF16)] * 2 + [pltpu.SemaphoreType.DMA((2,))],
    )
    sums = lax.psum(tuple(terms), "local")
    back = call(
        functools.partial(outputs_kernel, parts),
        [HBM] * (len(sums) + 2),
        jax.ShapeDtypeStruct((rows, width), BF16),
        *in_hbm(*sums, up, down),
        scratch=[pltpu.VMEM((rows, hidden), BF16)] * 2
        + [pltpu.VMEM((feat, hidden), BF16)] * 2
        + [pltpu.SemaphoreType.DMA((len(sums) + 2,))],
        limit=32,
    )
    returned = exchange(back)
    mixed, d_tokens, d_gates = call(
        functools.partial(unpack_kernel, nodes, capacity),
        [VMEM] * 3,
        (
            jax.ShapeDtypeStruct((tok, feat), BF16),
            jax.ShapeDtypeStruct((tok, feat), BF16),
            jax.ShapeDtypeStruct((top, tok), F32),
        ),
        routes_t,
        gate_probs.T,
        returned,
    )
    return mixed, d_tokens, d_gates.T


def solution(mesh):
    in_specs = (
        P("node", "local"),
        P("node", "local"),
        P("node", None),
        P("node", None),
        P("node", "local", None),
        P("node", None, "local"),
    )
    out_specs = (P("node", "local"), P("node", "local"), P("node", None))
    return jax.shard_map(body, mesh=mesh, in_specs=in_specs, out_specs=out_specs, check_vma=False)
```

```python
import functools

import jax
import jax.numpy as jnp
from jax import lax
from jax.experimental import pallas as pl
from jax.experimental.pallas import tpu as pltpu
from jax.sharding import PartitionSpec as P

BF16 = jnp.bfloat16
F32 = jnp.float32
VMEM = pl.BlockSpec(memory_space=pltpu.VMEM)
HBM = pl.BlockSpec(memory_space=pltpu.HBM)


def pieces(rows, cols):
    out = [(r, 16, 0, cols) for r in range(0, rows, 16)]
    r, nr, _, _ = out.pop()
    return out + [(r, nr, 0, cols // 2), (r, nr, cols // 2, cols // 2)]


def slot_columns(routes, node_count, capacity):
    tok, top = routes.shape
    rows = node_count * capacity
    expert = lax.broadcasted_iota(jnp.int32, (tok, node_count), 1)
    hits = jnp.zeros((tok, node_count), F32)
    for k in range(top):
        hits += jnp.where(routes[:, k : k + 1] == expert, 1.0, 0.0)
    earlier = lax.broadcasted_iota(jnp.int32, (tok, tok), 1) < lax.broadcasted_iota(jnp.int32, (tok, tok), 0)
    before = jnp.dot(jnp.where(earlier, 1.0, 0.0).astype(BF16), hits.astype(BF16), preferred_element_type=F32)
    col = lax.broadcasted_iota(jnp.int32, (tok, rows), 1)
    spread = jnp.where(
        lax.broadcasted_iota(jnp.int32, (node_count, rows), 1) // capacity
        == lax.broadcasted_iota(jnp.int32, (node_count, rows), 0),
        1.0,
        0.0,
    ).astype(BF16)
    before_cols = jnp.dot(before.astype(BF16), spread, preferred_element_type=F32)
    in_slot = before_cols == (col % capacity).astype(F32)
    return col // capacity, in_slot


def pack_kernel(node_count, capacity, routes_ref, tokens_ref, cot_ref, sent_ref, tokens_buf, cot_buf, routes_buf, sems):
    copies = [
        pltpu.make_async_copy(tokens_ref, tokens_buf, sems.at[0]),
        pltpu.make_async_copy(cot_ref, cot_buf, sems.at[1]),
        pltpu.make_async_copy(routes_ref, routes_buf, sems.at[2]),
    ]
    for copy in copies[::-1]:
        copy.start()
    copies[2].wait()
    routes = routes_buf[...].T
    expert, in_slot = slot_columns(routes, node_count, capacity)
    chosen = jnp.zeros(expert.shape, F32)
    for k in range(routes.shape[1]):
        chosen += jnp.where((routes[:, k : k + 1] == expert) & in_slot, 1.0, 0.0)
    chosen = chosen.T.astype(BF16)
    for copy in copies[:2]:
        copy.wait()
    both = jnp.concatenate([tokens_buf[...].astype(F32), cot_buf[...].astype(F32)], axis=1).astype(BF16)
    sent_ref[...] = jnp.dot(chosen, both, preferred_element_type=F32).astype(BF16)


def terms_kernel(parts, x_ref, w_in_hbm, w_out_hbm, *refs):
    outs, (w_in_ref, w_out_ref, sems) = refs[: 2 * len(parts)], refs[2 * len(parts) :]
    weights = [
        pltpu.make_async_copy(w_in_hbm, w_in_ref, sems.at[0]),
        pltpu.make_async_copy(w_out_hbm, w_out_ref, sems.at[1]),
    ]
    for copy in weights:
        copy.start()
    feat = w_in_ref.shape[0]
    rows = x_ref.shape[0]
    step = min(128, rows)
    for r0 in range(0, rows, step):
        band = slice(r0, r0 + step)
        if r0 == 0:
            weights[0].wait()
        pre = jnp.dot(x_ref[band, :feat], w_in_ref[...], preferred_element_type=F32).astype(BF16)
        if r0 == 0:
            weights[1].wait()
        dact = jnp.dot(x_ref[band, feat:], w_out_ref[...], preferred_element_type=F32).astype(BF16)
        for value, refs in ((pre, outs[: len(parts)]), (dact, outs[len(parts) :])):
            for (r, nr, c, nc), ref in zip(parts, refs):
                if r0 <= r < r0 + step:
                    ref[...] = value[r - r0 : r - r0 + nr, c : c + nc]


def outputs_kernel(parts, *refs):
    count = len(parts)
    sums = refs[: 2 * count]
    w_in_hbm, w_out_hbm, back_ref, pre_ref, dact_ref, w_in_ref, w_out_ref, sems = refs[2 * count :]
    feat = w_in_ref.shape[0]
    rows, width = back_ref.shape
    half = width // 2
    step = min(128, rows)
    copies = [
        (r, pltpu.make_async_copy(sums[first + i], target.at[pl.ds(r, nr), pl.ds(c, nc)], sems.at[first + i]))
        for i, (r, nr, c, nc) in enumerate(parts)
        for first, target in ((0, pre_ref), (count, dact_ref))
    ]
    weights = [
        pltpu.make_async_copy(w_out_hbm, w_out_ref, sems.at[2 * count]),
        pltpu.make_async_copy(w_in_hbm, w_in_ref, sems.at[2 * count + 1]),
    ]
    for copy in [copy for r, copy in copies if r < step] + weights + [copy for r, copy in copies if r >= step]:
        copy.start()

    for r0 in range(0, rows, step):
        for r, copy in copies:
            if r0 <= r < r0 + step:
                copy.wait()
        band = slice(r0, r0 + step)
        pre = pre_ref[band].astype(F32)
        dact = dact_ref[band].astype(F32)
        sig = 0.5 * jnp.tanh(0.5 * pre) + 0.5
        silu = pre * sig
        act = silu.astype(BF16)
        dpre = (dact * (sig + silu * (1.0 - sig))).astype(BF16)
        inner = jnp.sum(act.astype(F32) * dact, axis=1, keepdims=True)
        hi = inner.astype(BF16).astype(F32)
        mid = (inner - hi).astype(BF16).astype(F32)
        lo = inner - hi - mid
        if r0 == 0:
            for copy in weights:
                copy.wait()
        y = lax.dot_general(act, w_out_ref[...], (((1,), (1,)), ((), ())), preferred_element_type=F32)
        dout = lax.dot_general(dpre, w_in_ref[...], (((1,), (1,)), ((), ())), preferred_element_type=F32)
        lane = lax.broadcasted_iota(jnp.int32, (step, half - feat), 1)
        extra = jnp.where(lane == 0, hi, jnp.where(lane == 1, mid, jnp.where(lane == 2, lo, 0.0)))
        back_ref[band, :feat] = y.astype(BF16)
        back_ref[band, feat:half] = extra.astype(BF16)
        back_ref[band, half : half + feat] = dout.astype(BF16)
        back_ref[band, half + feat :] = jnp.zeros((step, half - feat), BF16)


def unpack_kernel(node_count, capacity, routes_ref, gates_ref, back_ref, mixed_ref, d_tokens_ref, d_gates_ref):
    routes = routes_ref[...].T
    gates = gates_ref[...].T
    tok, top = routes.shape
    feat = mixed_ref.shape[1]
    half = back_ref.shape[1] // 2
    expert, in_slot = slot_columns(routes, node_count, capacity)
    weight = jnp.zeros(expert.shape, F32)
    picks = []
    for k in range(top):
        mine = (routes[:, k : k + 1] == expert) & in_slot
        weight += jnp.where(mine, gates[:, k : k + 1], 0.0)
        picks.append(jnp.where(mine, 1.0, 0.0).astype(BF16))
    hi = weight.astype(BF16)
    rest = weight - hi.astype(F32)
    mid = rest.astype(BF16)
    lo = (rest - mid.astype(F32)).astype(BF16)
    stack = jnp.concatenate([hi, mid, lo], axis=0)
    out = jnp.dot(stack, back_ref[...], preferred_element_type=F32)
    out = out[:tok] + (out[tok : 2 * tok] + out[2 * tok :])
    mixed_ref[...] = out[:, :feat].astype(BF16)
    d_tokens_ref[...] = out[:, half : half + feat].astype(BF16)
    tail = half - 128
    lane = lax.broadcasted_iota(jnp.int32, (1, 128), 1)
    column = lax.broadcasted_iota(jnp.int32, (tok, top), 1)
    d_gates = jnp.zeros((tok, top), F32)
    for k in range(top):
        got = jnp.dot(picks[k], back_ref[:, tail:half], preferred_element_type=F32)
        value = jnp.sum(jnp.where(lane >= feat - tail, got, 0.0), axis=1, keepdims=True)
        d_gates = jnp.where(column == k, value, d_gates)
    d_gates_ref[...] = d_gates.T


def call(kernel, in_specs, out_shape, *args, scratch=(), limit=16):
    return pl.pallas_call(
        kernel,
        out_shape=out_shape,
        in_specs=in_specs,
        out_specs=jax.tree.map(lambda _: VMEM, out_shape),
        scratch_shapes=scratch,
        compiler_params=pltpu.CompilerParams(vmem_limit_bytes=limit * 1024 * 1024),
    )(*args)


def in_hbm(*arrays):
    return [pltpu.with_memory_space_constraint(array, pltpu.HBM) for array in arrays]


def body(tokens, cotangent, routes, gate_probs, w_in, w_out):
    tok, feat = tokens.shape
    top = routes.shape[1]
    nodes = lax.axis_size("node")
    hidden = w_in.shape[2]
    capacity = min(tok, 2 * tok * top // nodes)
    rows = nodes * capacity
    width = 2 * (-(-(feat + 3) // 128) * 128)
    parts = pieces(rows, hidden)
    up, down = w_in[0], w_out[0].T
    routes_t = routes.T

    def exchange(values):
        return lax.all_to_all(
            values.reshape(nodes, capacity, values.shape[1]), "node", split_axis=0, concat_axis=0, tiled=True
        ).reshape(rows, values.shape[1])

    sent = call(
        functools.partial(pack_kernel, nodes, capacity),
        [HBM] * 3,
        jax.ShapeDtypeStruct((rows, 2 * feat), BF16),
        *in_hbm(routes_t, tokens, cotangent),
        scratch=[pltpu.VMEM((tok, feat), BF16)] * 2
        + [pltpu.VMEM((top, tok), jnp.int32), pltpu.SemaphoreType.DMA((3,))],
    )
    x_dy = exchange(sent)
    terms = call(
        functools.partial(terms_kernel, parts),
        [VMEM, HBM, HBM],
        tuple(pltpu.VMEM((nr, nc), BF16) for _, nr, _, nc in parts) * 2,
        x_dy,
        *in_hbm(up, down),
        scratch=[pltpu.VMEM((feat, hidden), BF16)] * 2 + [pltpu.SemaphoreType.DMA((2,))],
    )
    sums = lax.psum(tuple(terms), "local")
    back = call(
        functools.partial(outputs_kernel, parts),
        [HBM] * (len(sums) + 2),
        jax.ShapeDtypeStruct((rows, width), BF16),
        *in_hbm(*sums, up, down),
        scratch=[pltpu.VMEM((rows, hidden), BF16)] * 2
        + [pltpu.VMEM((feat, hidden), BF16)] * 2
        + [pltpu.SemaphoreType.DMA((len(sums) + 2,))],
        limit=32,
    )
    returned = exchange(back)
    mixed, d_tokens, d_gates = call(
        functools.partial(unpack_kernel, nodes, capacity),
        [VMEM] * 3,
        (
            jax.ShapeDtypeStruct((tok, feat), BF16),
            jax.ShapeDtypeStruct((tok, feat), BF16),
            jax.ShapeDtypeStruct((top, tok), F32),
        ),
        routes_t,
        gate_probs.T,
        returned,
    )
    return mixed, d_tokens, d_gates.T


def solution(mesh):
    in_specs = (
        P("node", "local"),
        P("node", "local"),
        P("node", None),
        P("node", None),
        P("node", "local", None),
        P("node", None, "local"),
    )
    out_specs = (P("node", "local"), P("node", "local"), P("node", None))
    return jax.shard_map(body, mesh=mesh, in_specs=in_specs, out_specs=out_specs, check_vma=False)
```

```python
import functools

import jax
import jax.numpy as jnp
from jax import lax
from jax.experimental import pallas as pl
from jax.experimental.pallas import tpu as pltpu
from jax.sharding import PartitionSpec as P

BF16 = jnp.bfloat16
F32 = jnp.float32
VMEM = pl.BlockSpec(memory_space=pltpu.VMEM)
HBM = pl.BlockSpec(memory_space=pltpu.HBM)


def pieces(rows, cols):
    out = [(r, 16, 0, cols) for r in range(0, rows, 16)]
    r, nr, _, _ = out.pop()
    return out + [(r, nr, 0, cols // 2), (r, nr, cols // 2, cols // 2)]


def slot_columns(routes, node_count, capacity):
    tok, top = routes.shape
    rows = node_count * capacity
    expert = lax.broadcasted_iota(jnp.int32, (tok, node_count), 1)
    hits = jnp.zeros((tok, node_count), F32)
    for k in range(top):
        hits += jnp.where(routes[:, k : k + 1] == expert, 1.0, 0.0)
    earlier = lax.broadcasted_iota(jnp.int32, (tok, tok), 1) < lax.broadcasted_iota(jnp.int32, (tok, tok), 0)
    before = jnp.dot(jnp.where(earlier, 1.0, 0.0).astype(BF16), hits.astype(BF16), preferred_element_type=F32)
    col = lax.broadcasted_iota(jnp.int32, (tok, rows), 1)
    spread = jnp.where(
        lax.broadcasted_iota(jnp.int32, (node_count, rows), 1) // capacity
        == lax.broadcasted_iota(jnp.int32, (node_count, rows), 0),
        1.0,
        0.0,
    ).astype(BF16)
    before_cols = jnp.dot(before.astype(BF16), spread, preferred_element_type=F32)
    in_slot = before_cols == (col % capacity).astype(F32)
    return col // capacity, in_slot


def pack_kernel(node_count, capacity, routes_ref, tokens_ref, cot_ref, sent_ref, tokens_buf, cot_buf, routes_buf, sems):
    copies = [
        pltpu.make_async_copy(tokens_ref, tokens_buf, sems.at[0]),
        pltpu.make_async_copy(cot_ref, cot_buf, sems.at[1]),
        pltpu.make_async_copy(routes_ref, routes_buf, sems.at[2]),
    ]
    for copy in copies[::-1]:
        copy.start()
    copies[2].wait()
    routes = routes_buf[...].T
    expert, in_slot = slot_columns(routes, node_count, capacity)
    chosen = jnp.zeros(expert.shape, F32)
    for k in range(routes.shape[1]):
        chosen += jnp.where((routes[:, k : k + 1] == expert) & in_slot, 1.0, 0.0)
    chosen = chosen.T.astype(BF16)
    for copy in copies[:2]:
        copy.wait()
    both = jnp.concatenate([tokens_buf[...].astype(F32), cot_buf[...].astype(F32)], axis=1).astype(BF16)
    sent_ref[...] = jnp.dot(chosen, both, preferred_element_type=F32).astype(BF16)


def terms_kernel(parts, x_ref, w_in_hbm, w_out_hbm, *refs):
    outs, (w_in_ref, w_out_ref, sems) = refs[: 2 * len(parts)], refs[2 * len(parts) :]
    weights = [
        pltpu.make_async_copy(w_in_hbm, w_in_ref, sems.at[0]),
        pltpu.make_async_copy(w_out_hbm, w_out_ref, sems.at[1]),
    ]
    for copy in weights:
        copy.start()
    feat = w_in_ref.shape[0]
    rows = x_ref.shape[0]
    step = min(128, rows)
    sides = ((0, w_in_ref, outs[: len(parts)]), (feat, w_out_ref, outs[len(parts) :]))
    for (first, weight_ref, side_outs), copy in zip(sides, weights):
        copy.wait()
        for r0 in range(0, rows, step):
            value = jnp.dot(
                x_ref[r0 : r0 + step, first : first + feat], weight_ref[...], preferred_element_type=F32
            ).astype(BF16)
            for (r, nr, c, nc), ref in zip(parts, side_outs):
                if r0 <= r < r0 + step:
                    ref[...] = value[r - r0 : r - r0 + nr, c : c + nc]


def outputs_kernel(parts, *refs):
    count = len(parts)
    sums = refs[: 2 * count]
    w_in_hbm, w_out_hbm, back_ref, pre_ref, dact_ref, w_in_ref, w_out_ref, sems = refs[2 * count :]
    feat = w_in_ref.shape[0]
    rows, width = back_ref.shape
    half = width // 2
    step = min(256, rows)
    copies = [
        (r, pltpu.make_async_copy(sums[first + i], target.at[pl.ds(r, nr), pl.ds(c, nc)], sems.at[first + i]))
        for i, (r, nr, c, nc) in enumerate(parts)
        for first, target in ((0, pre_ref), (count, dact_ref))
    ]
    weights = [
        pltpu.make_async_copy(w_out_hbm, w_out_ref, sems.at[2 * count]),
        pltpu.make_async_copy(w_in_hbm, w_in_ref, sems.at[2 * count + 1]),
    ]
    for copy in [copy for r, copy in copies if r < step] + weights + [copy for r, copy in copies if r >= step]:
        copy.start()

    def activations(r0):
        for r, copy in copies:
            if r0 <= r < r0 + step:
                copy.wait()
        band = slice(r0, r0 + step)
        pre = pre_ref[band].astype(F32)
        dact = dact_ref[band].astype(F32)
        sig = 0.5 * jnp.tanh(0.5 * pre) + 0.5
        silu = pre * sig
        act = silu.astype(BF16)
        dpre = (dact * (sig + silu * (1.0 - sig))).astype(BF16)
        inner = jnp.sum(act.astype(F32) * dact, axis=1, keepdims=True)
        return act, dpre, inner

    ready = activations(0)
    for copy in weights:
        copy.wait()
    for r0 in range(0, rows, step):
        act, dpre, inner = ready
        if r0 + step < rows:
            ready = activations(r0 + step)
        band = slice(r0, r0 + step)
        hi = inner.astype(BF16).astype(F32)
        mid = (inner - hi).astype(BF16).astype(F32)
        lo = inner - hi - mid
        y = lax.dot_general(act, w_out_ref[...], (((1,), (1,)), ((), ())), preferred_element_type=F32)
        dout = lax.dot_general(dpre, w_in_ref[...], (((1,), (1,)), ((), ())), preferred_element_type=F32)
        lane = lax.broadcasted_iota(jnp.int32, (step, half - feat), 1)
        extra = jnp.where(lane == 0, hi, jnp.where(lane == 1, mid, jnp.where(lane == 2, lo, 0.0)))
        back_ref[band, :feat] = y.astype(BF16)
        back_ref[band, feat:half] = extra.astype(BF16)
        back_ref[band, half : half + feat] = dout.astype(BF16)
        back_ref[band, half + feat :] = jnp.zeros((step, half - feat), BF16)


def places_kernel(node_count, capacity, routes_ref, gates_ref, stack_ref):
    routes = routes_ref[...].T
    gates = gates_ref[...].T
    tok, top = routes.shape
    expert, in_slot = slot_columns(routes, node_count, capacity)
    weight = jnp.zeros(expert.shape, F32)
    for k in range(top):
        mine = (routes[:, k : k + 1] == expert) & in_slot
        weight += jnp.where(mine, gates[:, k : k + 1], 0.0)
        stack_ref[(3 + k) * tok : (4 + k) * tok] = jnp.where(mine, 1.0, 0.0).astype(BF16)
    hi = weight.astype(BF16)
    rest = weight - hi.astype(F32)
    mid = rest.astype(BF16)
    stack_ref[:tok] = hi
    stack_ref[tok : 2 * tok] = mid
    stack_ref[2 * tok : 3 * tok] = (rest - mid.astype(F32)).astype(BF16)


def unpack_kernel(stack_ref, back_ref, mixed_ref, d_tokens_ref, d_gates_ref):
    tok, feat = mixed_ref.shape
    top = d_gates_ref.shape[0]
    half = back_ref.shape[1] // 2
    out = jnp.dot(stack_ref[: 3 * tok], back_ref[...], preferred_element_type=F32)
    out = out[:tok] + (out[tok : 2 * tok] + out[2 * tok :])
    mixed_ref[...] = out[:, :feat].astype(BF16)
    d_tokens_ref[...] = out[:, half : half + feat].astype(BF16)
    tail = half - 128
    lane = lax.broadcasted_iota(jnp.int32, (1, 128), 1)
    column = lax.broadcasted_iota(jnp.int32, (tok, top), 1)
    got = jnp.dot(stack_ref[3 * tok :], back_ref[:, tail:half], preferred_element_type=F32)
    values = jnp.sum(jnp.where(lane >= feat - tail, got, 0.0), axis=1, keepdims=True)
    d_gates = jnp.zeros((tok, top), F32)
    for k in range(top):
        d_gates = jnp.where(column == k, values[k * tok : (k + 1) * tok], d_gates)
    d_gates_ref[...] = d_gates.T


def call(kernel, in_specs, out_shape, *args, scratch=(), limit=16):
    return pl.pallas_call(
        kernel,
        out_shape=out_shape,
        in_specs=in_specs,
        out_specs=jax.tree.map(lambda _: VMEM, out_shape),
        scratch_shapes=scratch,
        compiler_params=pltpu.CompilerParams(vmem_limit_bytes=limit * 1024 * 1024),
    )(*args)


def in_hbm(*arrays):
    return [pltpu.with_memory_space_constraint(array, pltpu.HBM) for array in arrays]


def body(tokens, cotangent, routes, gate_probs, w_in, w_out):
    tok, feat = tokens.shape
    top = routes.shape[1]
    nodes = lax.axis_size("node")
    hidden = w_in.shape[2]
    capacity = min(tok, 2 * tok * top // nodes)
    rows = nodes * capacity
    width = 2 * (-(-(feat + 3) // 128) * 128)
    parts = pieces(rows, hidden)
    up, down = w_in[0], w_out[0].T
    routes_t = routes.T

    def exchange(values):
        return lax.all_to_all(
            values.reshape(nodes, capacity, values.shape[1]), "node", split_axis=0, concat_axis=0, tiled=True
        ).reshape(rows, values.shape[1])

    sent = call(
        functools.partial(pack_kernel, nodes, capacity),
        [HBM] * 3,
        jax.ShapeDtypeStruct((rows, 2 * feat), BF16),
        *in_hbm(routes_t, tokens, cotangent),
        scratch=[pltpu.VMEM((tok, feat), BF16)] * 2
        + [pltpu.VMEM((top, tok), jnp.int32), pltpu.SemaphoreType.DMA((3,))],
    )
    x_dy = exchange(sent)
    terms = call(
        functools.partial(terms_kernel, parts),
        [VMEM, HBM, HBM],
        tuple(pltpu.VMEM((nr, nc), BF16) for _, nr, _, nc in parts) * 2,
        x_dy,
        *in_hbm(up, down),
        scratch=[pltpu.VMEM((feat, hidden), BF16)] * 2 + [pltpu.SemaphoreType.DMA((2,))],
    )
    sums = lax.psum(tuple(terms), "local")
    back = call(
        functools.partial(outputs_kernel, parts),
        [HBM] * (len(sums) + 2),
        jax.ShapeDtypeStruct((rows, width), BF16),
        *in_hbm(*sums, up, down),
        scratch=[pltpu.VMEM((rows, hidden), BF16)] * 2
        + [pltpu.VMEM((feat, hidden), BF16)] * 2
        + [pltpu.SemaphoreType.DMA((len(sums) + 2,))],
        limit=32,
    )
    late_routes, late_gates, back = lax.optimization_barrier((routes_t, gate_probs.T, back))
    places = call(
        functools.partial(places_kernel, nodes, capacity),
        [VMEM] * 2,
        jax.ShapeDtypeStruct(((3 + top) * tok, rows), BF16),
        late_routes,
        late_gates,
    )
    returned = exchange(back)
    mixed, d_tokens, d_gates = call(
        unpack_kernel,
        [VMEM] * 2,
        (
            jax.ShapeDtypeStruct((tok, feat), BF16),
            jax.ShapeDtypeStruct((tok, feat), BF16),
            jax.ShapeDtypeStruct((top, tok), F32),
        ),
        places,
        returned,
    )
    return mixed, d_tokens, d_gates.T


def solution(mesh):
    in_specs = (
        P("node", "local"),
        P("node", "local"),
        P("node", None),
        P("node", None),
        P("node", "local", None),
        P("node", None, "local"),
    )
    out_specs = (P("node", "local"), P("node", "local"), P("node", None))
    return jax.shard_map(body, mesh=mesh, in_specs=in_specs, out_specs=out_specs, check_vma=False)
```

```python
import functools

import jax
import jax.numpy as jnp
from jax import lax
from jax.experimental import pallas as pl
from jax.experimental.pallas import tpu as pltpu
from jax.sharding import PartitionSpec as P

BF16 = jnp.bfloat16
F32 = jnp.float32
VMEM = pl.BlockSpec(memory_space=pltpu.VMEM)
HBM = pl.BlockSpec(memory_space=pltpu.HBM)


def pieces(rows, cols):
    out = [(r, 16, 0, cols) for r in range(0, rows, 16)]
    r, nr, _, _ = out.pop()
    return out + [(r, nr, 0, cols // 2), (r, nr, cols // 2, cols // 2)]


def slot_columns(routes, node_count, capacity):
    tok, top = routes.shape
    rows = node_count * capacity
    expert = lax.broadcasted_iota(jnp.int32, (tok, node_count), 1)
    hits = jnp.zeros((tok, node_count), F32)
    for k in range(top):
        hits += jnp.where(routes[:, k : k + 1] == expert, 1.0, 0.0)
    earlier = lax.broadcasted_iota(jnp.int32, (tok, tok), 1) < lax.broadcasted_iota(jnp.int32, (tok, tok), 0)
    before = jnp.dot(jnp.where(earlier, 1.0, 0.0).astype(BF16), hits.astype(BF16), preferred_element_type=F32)
    col = lax.broadcasted_iota(jnp.int32, (tok, rows), 1)
    spread = jnp.where(
        lax.broadcasted_iota(jnp.int32, (node_count, rows), 1) // capacity
        == lax.broadcasted_iota(jnp.int32, (node_count, rows), 0),
        1.0,
        0.0,
    ).astype(BF16)
    before_cols = jnp.dot(before.astype(BF16), spread, preferred_element_type=F32)
    in_slot = before_cols == (col % capacity).astype(F32)
    return col // capacity, in_slot


def pack_kernel(node_count, capacity, routes_ref, tokens_ref, cot_ref, sent_ref, tokens_buf, cot_buf, routes_buf, sems):
    copies = [
        pltpu.make_async_copy(tokens_ref, tokens_buf, sems.at[0]),
        pltpu.make_async_copy(cot_ref, cot_buf, sems.at[1]),
        pltpu.make_async_copy(routes_ref, routes_buf, sems.at[2]),
    ]
    for copy in copies[::-1]:
        copy.start()
    copies[2].wait()
    routes = routes_buf[...].T
    expert, in_slot = slot_columns(routes, node_count, capacity)
    chosen = jnp.zeros(expert.shape, F32)
    for k in range(routes.shape[1]):
        chosen += jnp.where((routes[:, k : k + 1] == expert) & in_slot, 1.0, 0.0)
    chosen = chosen.T.astype(BF16)
    for copy in copies[:2]:
        copy.wait()
    both = jnp.concatenate([tokens_buf[...].astype(F32), cot_buf[...].astype(F32)], axis=1).astype(BF16)
    sent_ref[...] = jnp.dot(chosen, both, preferred_element_type=F32).astype(BF16)


def terms_kernel(parts, x_ref, w_in_hbm, w_out_hbm, *refs):
    outs, (w_in_ref, w_out_ref, sems) = refs[: 2 * len(parts)], refs[2 * len(parts) :]
    weights = [
        pltpu.make_async_copy(w_in_hbm, w_in_ref, sems.at[0]),
        pltpu.make_async_copy(w_out_hbm, w_out_ref, sems.at[1]),
    ]
    for copy in weights:
        copy.start()
    feat = w_in_ref.shape[0]
    rows = x_ref.shape[0]
    step = min(128, rows)
    sides = ((0, w_in_ref, outs[: len(parts)]), (feat, w_out_ref, outs[len(parts) :]))
    for (first, weight_ref, side_outs), copy in zip(sides, weights):
        copy.wait()
        for r0 in range(0, rows, step):
            value = jnp.dot(
                x_ref[r0 : r0 + step, first : first + feat], weight_ref[...], preferred_element_type=F32
            ).astype(BF16)
            for (r, nr, c, nc), ref in zip(parts, side_outs):
                if r0 <= r < r0 + step:
                    ref[...] = value[r - r0 : r - r0 + nr, c : c + nc]


def outputs_kernel(parts, near, *refs):
    count = len(parts)
    sums = refs[: 2 * count]
    w_in_hbm, w_out_hbm, back_ref, pre_ref, dact_ref, w_in_ref, w_out_ref, sems = refs[2 * count :]
    feat = w_in_ref.shape[0]
    rows, width = back_ref.shape
    half = width // 2
    step = min(256, rows)
    copies = [
        (r, pltpu.make_async_copy(sums[first + i], target.at[pl.ds(r, nr), pl.ds(c, nc)], sems.at[first + i]))
        for i, (r, nr, c, nc) in enumerate(parts)
        for first, target in ((0, pre_ref), (count, dact_ref))
        if i >= near
    ]
    weights = [
        pltpu.make_async_copy(w_out_hbm, w_out_ref, sems.at[2 * count]),
        pltpu.make_async_copy(w_in_hbm, w_in_ref, sems.at[2 * count + 1]),
    ]
    for copy in [copy for r, copy in copies if r < step] + weights + [copy for r, copy in copies if r >= step]:
        copy.start()

    def band_of(r0, first, held):
        values = [sums[first + i][...] for i, (r, _, _, _) in enumerate(parts[:near]) if r0 <= r < r0 + step]
        done = r0 + sum(value.shape[0] for value in values)
        if done < r0 + step:
            values.append(held[done : r0 + step])
        return jnp.concatenate(values, axis=0).astype(F32)

    def activations(r0):
        for r, copy in copies:
            if r0 <= r < r0 + step:
                copy.wait()
        pre = band_of(r0, 0, pre_ref)
        dact = band_of(r0, count, dact_ref)
        sig = 0.5 * jnp.tanh(0.5 * pre) + 0.5
        silu = pre * sig
        act = silu.astype(BF16)
        dpre = (dact * (sig + silu * (1.0 - sig))).astype(BF16)
        inner = jnp.sum(act.astype(F32) * dact, axis=1, keepdims=True)
        return act, dpre, inner

    ready = activations(0)
    for copy in weights:
        copy.wait()
    for r0 in range(0, rows, step):
        act, dpre, inner = ready
        if r0 + step < rows:
            ready = activations(r0 + step)
        band = slice(r0, r0 + step)
        hi = inner.astype(BF16).astype(F32)
        mid = (inner - hi).astype(BF16).astype(F32)
        lo = inner - hi - mid
        y = lax.dot_general(act, w_out_ref[...], (((1,), (1,)), ((), ())), preferred_element_type=F32)
        dout = lax.dot_general(dpre, w_in_ref[...], (((1,), (1,)), ((), ())), preferred_element_type=F32)
        lane = lax.broadcasted_iota(jnp.int32, (step, half - feat), 1)
        extra = jnp.where(lane == 0, hi, jnp.where(lane == 1, mid, jnp.where(lane == 2, lo, 0.0)))
        back_ref[band, :feat] = y.astype(BF16)
        back_ref[band, feat:half] = extra.astype(BF16)
        back_ref[band, half : half + feat] = dout.astype(BF16)
        back_ref[band, half + feat :] = jnp.zeros((step, half - feat), BF16)


def places_kernel(node_count, capacity, routes_ref, gates_ref, stack_ref):
    routes = routes_ref[...].T
    gates = gates_ref[...].T
    tok, top = routes.shape
    expert, in_slot = slot_columns(routes, node_count, capacity)
    weight = jnp.zeros(expert.shape, F32)
    for k in range(top):
        mine = (routes[:, k : k + 1] == expert) & in_slot
        weight += jnp.where(mine, gates[:, k : k + 1], 0.0)
        stack_ref[(3 + k) * tok : (4 + k) * tok] = jnp.where(mine, 1.0, 0.0).astype(BF16)
    hi = weight.astype(BF16)
    rest = weight - hi.astype(F32)
    mid = rest.astype(BF16)
    stack_ref[:tok] = hi
    stack_ref[tok : 2 * tok] = mid
    stack_ref[2 * tok : 3 * tok] = (rest - mid.astype(F32)).astype(BF16)


def unpack_kernel(stack_ref, back_ref, mixed_ref, d_tokens_ref, d_gates_ref):
    tok, feat = mixed_ref.shape
    top = d_gates_ref.shape[0]
    half = back_ref.shape[1] // 2
    out = jnp.dot(stack_ref[: 3 * tok], back_ref[...], preferred_element_type=F32)
    out = out[:tok] + (out[tok : 2 * tok] + out[2 * tok :])
    mixed_ref[...] = out[:, :feat].astype(BF16)
    d_tokens_ref[...] = out[:, half : half + feat].astype(BF16)
    tail = half - 128
    lane = lax.broadcasted_iota(jnp.int32, (1, 128), 1)
    column = lax.broadcasted_iota(jnp.int32, (tok, top), 1)
    got = jnp.dot(stack_ref[3 * tok :], back_ref[:, tail:half], preferred_element_type=F32)
    values = jnp.sum(jnp.where(lane >= feat - tail, got, 0.0), axis=1, keepdims=True)
    d_gates = jnp.zeros((tok, top), F32)
    for k in range(top):
        d_gates = jnp.where(column == k, values[k * tok : (k + 1) * tok], d_gates)
    d_gates_ref[...] = d_gates.T


def call(kernel, in_specs, out_shape, *args, scratch=(), limit=16):
    return pl.pallas_call(
        kernel,
        out_shape=out_shape,
        in_specs=in_specs,
        out_specs=jax.tree.map(lambda _: VMEM, out_shape),
        scratch_shapes=scratch,
        compiler_params=pltpu.CompilerParams(vmem_limit_bytes=limit * 1024 * 1024),
    )(*args)


def in_hbm(*arrays):
    return [pltpu.with_memory_space_constraint(array, pltpu.HBM) for array in arrays]


def body(tokens, cotangent, routes, gate_probs, w_in, w_out):
    tok, feat = tokens.shape
    top = routes.shape[1]
    nodes = lax.axis_size("node")
    hidden = w_in.shape[2]
    capacity = min(tok, 2 * tok * top // nodes)
    rows = nodes * capacity
    width = 2 * (-(-(feat + 3) // 128) * 128)
    parts = pieces(rows, hidden)
    up, down = w_in[0], w_out[0].T
    routes_t = routes.T

    def exchange(values):
        return lax.all_to_all(
            values.reshape(nodes, capacity, values.shape[1]), "node", split_axis=0, concat_axis=0, tiled=True
        ).reshape(rows, values.shape[1])

    sent = call(
        functools.partial(pack_kernel, nodes, capacity),
        [HBM] * 3,
        jax.ShapeDtypeStruct((rows, 2 * feat), BF16),
        *in_hbm(routes_t, tokens, cotangent),
        scratch=[pltpu.VMEM((tok, feat), BF16)] * 2
        + [pltpu.VMEM((top, tok), jnp.int32), pltpu.SemaphoreType.DMA((3,))],
    )
    x_dy = exchange(sent)
    terms = call(
        functools.partial(terms_kernel, parts),
        [VMEM, HBM, HBM],
        tuple(pltpu.VMEM((nr, nc), BF16) for _, nr, _, nc in parts) * 2,
        x_dy,
        *in_hbm(up, down),
        scratch=[pltpu.VMEM((feat, hidden), BF16)] * 2 + [pltpu.SemaphoreType.DMA((2,))],
    )
    sums = lax.psum(tuple(terms), "local")
    near = (len(parts) - 1) // 2
    spaces = [VMEM if i % len(parts) < near else HBM for i in range(len(sums))]
    placed = [pltpu.with_memory_space_constraint(part, spec.memory_space) for part, spec in zip(sums, spaces)]
    back = call(
        functools.partial(outputs_kernel, parts, near),
        spaces + [HBM] * 2,
        jax.ShapeDtypeStruct((rows, width), BF16),
        *placed,
        *in_hbm(up, down),
        scratch=[pltpu.VMEM((rows, hidden), BF16)] * 2
        + [pltpu.VMEM((feat, hidden), BF16)] * 2
        + [pltpu.SemaphoreType.DMA((len(sums) + 2,))],
        limit=32,
    )
    late_routes, late_gates, back = lax.optimization_barrier((routes_t, gate_probs.T, back))
    places = call(
        functools.partial(places_kernel, nodes, capacity),
        [VMEM] * 2,
        jax.ShapeDtypeStruct(((3 + top) * tok, rows), BF16),
        late_routes,
        late_gates,
    )
    returned = exchange(back)
    mixed, d_tokens, d_gates = call(
        unpack_kernel,
        [VMEM] * 2,
        (
            jax.ShapeDtypeStruct((tok, feat), BF16),
            jax.ShapeDtypeStruct((tok, feat), BF16),
            jax.ShapeDtypeStruct((top, tok), F32),
        ),
        places,
        returned,
    )
    return mixed, d_tokens, d_gates.T


def solution(mesh):
    in_specs = (
        P("node", "local"),
        P("node", "local"),
        P("node", None),
        P("node", None),
        P("node", "local", None),
        P("node", None, "local"),
    )
    out_specs = (P("node", "local"), P("node", "local"), P("node", None))
    return jax.shard_map(body, mesh=mesh, in_specs=in_specs, out_specs=out_specs, check_vma=False)
```

```python
import functools

import jax
import jax.numpy as jnp
from jax import lax
from jax.experimental import pallas as pl
from jax.experimental.pallas import tpu as pltpu
from jax.sharding import PartitionSpec as P

BF16 = jnp.bfloat16
F32 = jnp.float32
VMEM = pl.BlockSpec(memory_space=pltpu.VMEM)
HBM = pl.BlockSpec(memory_space=pltpu.HBM)


def pieces(rows, cols):
    out = [(r, 16, 0, cols) for r in range(0, rows, 16)]
    r, nr, _, _ = out.pop()
    return out + [(r, nr, 0, cols // 2), (r, nr, cols // 2, cols // 2)]


def slot_columns(routes, node_count, capacity):
    tok, top = routes.shape
    rows = node_count * capacity
    expert = lax.broadcasted_iota(jnp.int32, (tok, node_count), 1)
    hits = jnp.zeros((tok, node_count), F32)
    for k in range(top):
        hits += jnp.where(routes[:, k : k + 1] == expert, 1.0, 0.0)
    earlier = lax.broadcasted_iota(jnp.int32, (tok, tok), 1) < lax.broadcasted_iota(jnp.int32, (tok, tok), 0)
    before = jnp.dot(jnp.where(earlier, 1.0, 0.0).astype(BF16), hits.astype(BF16), preferred_element_type=F32)
    col = lax.broadcasted_iota(jnp.int32, (tok, rows), 1)
    spread = jnp.where(
        lax.broadcasted_iota(jnp.int32, (node_count, rows), 1) // capacity
        == lax.broadcasted_iota(jnp.int32, (node_count, rows), 0),
        1.0,
        0.0,
    ).astype(BF16)
    before_cols = jnp.dot(before.astype(BF16), spread, preferred_element_type=F32)
    in_slot = before_cols == (col % capacity).astype(F32)
    return col // capacity, in_slot


def pack_kernel(node_count, capacity, routes_ref, tokens_ref, cot_ref, sent_ref, tokens_buf, cot_buf, routes_buf, sems):
    copies = [
        pltpu.make_async_copy(tokens_ref, tokens_buf, sems.at[0]),
        pltpu.make_async_copy(cot_ref, cot_buf, sems.at[1]),
        pltpu.make_async_copy(routes_ref, routes_buf, sems.at[2]),
    ]
    for copy in copies[::-1]:
        copy.start()
    copies[2].wait()
    routes = routes_buf[...].T
    expert, in_slot = slot_columns(routes, node_count, capacity)
    chosen = jnp.zeros(expert.shape, F32)
    for k in range(routes.shape[1]):
        chosen += jnp.where((routes[:, k : k + 1] == expert) & in_slot, 1.0, 0.0)
    chosen = chosen.T.astype(BF16)
    for copy in copies[:2]:
        copy.wait()
    both = jnp.concatenate([tokens_buf[...].astype(F32), cot_buf[...].astype(F32)], axis=1).astype(BF16)
    sent_ref[...] = jnp.dot(chosen, both, preferred_element_type=F32).astype(BF16)


def terms_kernel(parts, x_ref, w_in_hbm, w_out_hbm, *refs):
    outs, (w_in_ref, w_out_ref, sems) = refs[: 2 * len(parts)], refs[2 * len(parts) :]
    weights = [
        pltpu.make_async_copy(w_in_hbm, w_in_ref, sems.at[0]),
        pltpu.make_async_copy(w_out_hbm, w_out_ref, sems.at[1]),
    ]
    for copy in weights:
        copy.start()
    feat = w_in_ref.shape[0]
    rows = x_ref.shape[0]
    step = min(128, rows)
    sides = ((0, w_in_ref, outs[: len(parts)]), (feat, w_out_ref, outs[len(parts) :]))
    for (first, weight_ref, side_outs), copy in zip(sides, weights):
        copy.wait()
        for r0 in range(0, rows, step):
            value = jnp.dot(
                x_ref[r0 : r0 + step, first : first + feat], weight_ref[...], preferred_element_type=F32
            ).astype(BF16)
            for (r, nr, c, nc), ref in zip(parts, side_outs):
                if r0 <= r < r0 + step:
                    ref[...] = value[r - r0 : r - r0 + nr, c : c + nc]


def outputs_kernel(parts, *refs):
    count = len(parts)
    sums = refs[: 2 * count]
    w_in_hbm, w_out_hbm, back_ref, pre_ref, dact_ref, w_in_ref, w_out_ref, sems = refs[2 * count :]
    feat = w_in_ref.shape[0]
    rows, width = back_ref.shape
    half = width // 2
    step = min(256, rows)
    copies = [
        (r, pltpu.make_async_copy(sums[first + i], target.at[pl.ds(r, nr), pl.ds(c, nc)], sems.at[first + i]))
        for i, (r, nr, c, nc) in enumerate(parts)
        for first, target in ((0, pre_ref), (count, dact_ref))
    ]
    weights = [
        pltpu.make_async_copy(w_out_hbm, w_out_ref, sems.at[2 * count]),
        pltpu.make_async_copy(w_in_hbm, w_in_ref, sems.at[2 * count + 1]),
    ]
    for copy in [copy for r, copy in copies if r < step] + weights + [copy for r, copy in copies if r >= step]:
        copy.start()

    def activations(r0):
        for r, copy in copies:
            if r0 <= r < r0 + step:
                copy.wait()
        band = slice(r0, r0 + step)
        pre = pre_ref[band].astype(F32)
        dact = dact_ref[band].astype(F32)
        sig = 0.5 * jnp.tanh(0.5 * pre) + 0.5
        silu = pre * sig
        act = silu.astype(BF16)
        dpre = (dact * (sig + silu * (1.0 - sig))).astype(BF16)
        inner = jnp.sum(act.astype(F32) * dact, axis=1, keepdims=True)
        return act, dpre, inner

    ready = activations(0)
    for copy in weights:
        copy.wait()
    for r0 in range(0, rows, step):
        act, dpre, inner = ready
        if r0 + step < rows:
            ready = activations(r0 + step)
        band = slice(r0, r0 + step)
        hi = inner.astype(BF16).astype(F32)
        mid = (inner - hi).astype(BF16).astype(F32)
        lo = inner - hi - mid
        y = lax.dot_general(act, w_out_ref[...], (((1,), (1,)), ((), ())), preferred_element_type=F32)
        dout = lax.dot_general(dpre, w_in_ref[...], (((1,), (1,)), ((), ())), preferred_element_type=F32)
        lane = lax.broadcasted_iota(jnp.int32, (step, half - feat), 1)
        extra = jnp.where(lane == 0, hi, jnp.where(lane == 1, mid, jnp.where(lane == 2, lo, 0.0)))
        back_ref[band, :feat] = y.astype(BF16)
        back_ref[band, feat:half] = extra.astype(BF16)
        back_ref[band, half : half + feat] = dout.astype(BF16)
        back_ref[band, half + feat :] = jnp.zeros((step, half - feat), BF16)


def places_kernel(node_count, capacity, routes_ref, gates_ref, stack_ref):
    routes = routes_ref[...].T
    gates = gates_ref[...].T
    tok, top = routes.shape
    expert, in_slot = slot_columns(routes, node_count, capacity)
    weight = jnp.zeros(expert.shape, F32)
    for k in range(top):
        mine = (routes[:, k : k + 1] == expert) & in_slot
        weight += jnp.where(mine, gates[:, k : k + 1], 0.0)
        stack_ref[(3 + k) * tok : (4 + k) * tok] = jnp.where(mine, 1.0, 0.0).astype(BF16)
    hi = weight.astype(BF16)
    rest = weight - hi.astype(F32)
    mid = rest.astype(BF16)
    stack_ref[:tok] = hi
    stack_ref[tok : 2 * tok] = mid
    stack_ref[2 * tok : 3 * tok] = (rest - mid.astype(F32)).astype(BF16)


def unpack_kernel(stack_ref, back_ref, mixed_ref, d_tokens_ref, d_gates_ref):
    tok, feat = mixed_ref.shape
    top = d_gates_ref.shape[0]
    half = back_ref.shape[1] // 2
    out = jnp.dot(stack_ref[: 3 * tok], back_ref[...], preferred_element_type=F32)
    out = out[:tok] + (out[tok : 2 * tok] + out[2 * tok :])
    mixed_ref[...] = out[:, :feat].astype(BF16)
    d_tokens_ref[...] = out[:, half : half + feat].astype(BF16)
    tail = half - 128
    lane = lax.broadcasted_iota(jnp.int32, (1, 128), 1)
    column = lax.broadcasted_iota(jnp.int32, (tok, top), 1)
    got = jnp.dot(stack_ref[3 * tok :], back_ref[:, tail:half], preferred_element_type=F32)
    values = jnp.sum(jnp.where(lane >= feat - tail, got, 0.0), axis=1, keepdims=True)
    d_gates = jnp.zeros((tok, top), F32)
    for k in range(top):
        d_gates = jnp.where(column == k, values[k * tok : (k + 1) * tok], d_gates)
    d_gates_ref[...] = d_gates.T


def call(kernel, in_specs, out_shape, *args, scratch=(), limit=16):
    return pl.pallas_call(
        kernel,
        out_shape=out_shape,
        in_specs=in_specs,
        out_specs=jax.tree.map(lambda _: VMEM, out_shape),
        scratch_shapes=scratch,
        compiler_params=pltpu.CompilerParams(vmem_limit_bytes=limit * 1024 * 1024),
    )(*args)


def in_hbm(*arrays):
    return [pltpu.with_memory_space_constraint(array, pltpu.HBM) for array in arrays]


def body(tokens, cotangent, routes, gate_probs, w_in, w_out):
    tok, feat = tokens.shape
    top = routes.shape[1]
    nodes = lax.axis_size("node")
    hidden = w_in.shape[2]
    capacity = min(tok, 2 * tok * top // nodes)
    rows = nodes * capacity
    width = 2 * (-(-(feat + 3) // 128) * 128)
    parts = pieces(rows, hidden)
    up, down = w_in[0], w_out[0].T
    routes_t = routes.T

    def exchange(values):
        return lax.all_to_all(
            values.reshape(nodes, capacity, values.shape[1]), "node", split_axis=0, concat_axis=0, tiled=True
        ).reshape(rows, values.shape[1])

    sent = call(
        functools.partial(pack_kernel, nodes, capacity),
        [HBM] * 3,
        jax.ShapeDtypeStruct((rows, 2 * feat), BF16),
        *in_hbm(routes_t, tokens, cotangent),
        scratch=[pltpu.VMEM((tok, feat), BF16)] * 2
        + [pltpu.VMEM((top, tok), jnp.int32), pltpu.SemaphoreType.DMA((3,))],
    )
    x_dy = exchange(sent)
    late_routes, late_gates, x_dy = lax.optimization_barrier((routes_t, gate_probs.T, x_dy))
    places = call(
        functools.partial(places_kernel, nodes, capacity),
        [VMEM] * 2,
        jax.ShapeDtypeStruct(((3 + top) * tok, rows), BF16),
        late_routes,
        late_gates,
    )
    places, x_dy = lax.optimization_barrier((places, x_dy))
    terms = call(
        functools.partial(terms_kernel, parts),
        [VMEM, HBM, HBM],
        tuple(pltpu.VMEM((nr, nc), BF16) for _, nr, _, nc in parts) * 2,
        x_dy,
        *in_hbm(up, down),
        scratch=[pltpu.VMEM((feat, hidden), BF16)] * 2 + [pltpu.SemaphoreType.DMA((2,))],
    )
    sums = lax.psum(tuple(terms), "local")
    back = call(
        functools.partial(outputs_kernel, parts),
        [HBM] * (len(sums) + 2),
        jax.ShapeDtypeStruct((rows, width), BF16),
        *in_hbm(*sums, up, down),
        scratch=[pltpu.VMEM((rows, hidden), BF16)] * 2
        + [pltpu.VMEM((feat, hidden), BF16)] * 2
        + [pltpu.SemaphoreType.DMA((len(sums) + 2,))],
        limit=32,
    )
    returned = exchange(back)
    mixed, d_tokens, d_gates = call(
        unpack_kernel,
        [VMEM] * 2,
        (
            jax.ShapeDtypeStruct((tok, feat), BF16),
            jax.ShapeDtypeStruct((tok, feat), BF16),
            jax.ShapeDtypeStruct((top, tok), F32),
        ),
        places,
        returned,
    )
    return mixed, d_tokens, d_gates.T


def solution(mesh):
    in_specs = (
        P("node", "local"),
        P("node", "local"),
        P("node", None),
        P("node", None),
        P("node", "local", None),
        P("node", None, "local"),
    )
    out_specs = (P("node", "local"), P("node", "local"), P("node", None))
    return jax.shard_map(body, mesh=mesh, in_specs=in_specs, out_specs=out_specs, check_vma=False)
```
